512 devices in a mesh: blk: 32 (over y_hi, x, core), fsdp: 16 (over z, y_lo).
Axes of the slice: x: 4, y: 8 (y_hi: 4, y_lo: 2; y = y_hi * 2 + y_lo), z: 8, core: 2. Of those that a mesh axis runs over, the one named last changes fastest.
Arguments:
- weights: bfloat16 [32, 12288, 1536], P('blk', 'fsdp'), may hold values from -9 to 9
- hidden: bfloat16 [32, 256, 12288], P('blk', None, 'fsdp'), may hold values from -6 to 6
- out_grad: bfloat16 [32, 256, 1536], P('blk', 'fsdp'), may hold values from -6 to 6
- q_start: float32 [32, 1536, 4], P('blk'), may hold values from -6 to 6
Outputs:
- new_weights: bfloat16 [32, 12288, 1536], P('blk', 'fsdp')
- edge_factors: float32 [32, 1536, 4], P('blk')
The draws below stay inside these ranges and needn't reach their ends.
All inputs are finite; a program needn't handle non-finite values.
Results may differ from the reference program's by a relative error of at most 0.013.
Values may be sent and summed in bfloat16 or wider, within the bound.
A program may use at most 64 MiB of HBM per device.

```python
import math
import jax
import jax.numpy as jnp
from jax import lax

D = 1536
FF = 12288
TOKENS = 256
R = 4
ROUNDS = 2
REPLICAS = 32


def row_scales(key, rise):
    position = jnp.arange(FF, dtype=jnp.float32) / max(FF - 1, 1)
    jitter = jnp.exp(jax.random.uniform(key, (REPLICAS, FF, 1), jnp.float32, -0.35, 0.35))
    return 0.2 * jnp.power(jnp.float32(rise), position)[None, :, None] * jitter


def draw_weights(key, part):
    key = jax.random.fold_in(key, 11)
    key_entries, key_rows = jax.random.split(key)
    entries = jnp.clip(jax.random.normal(key_entries, (REPLICAS, FF, D), jnp.float32), -3.0, 3.0)
    scales = row_scales(key_rows, 6.0)
    return (entries * scales).astype(jnp.bfloat16)


def level_of(key, extent, cuts, least, high):
    level, own = 1.0, jax.random.fold_in(key, 6)
    for axis_at, blocks in cuts:
        draws = jnp.exp(jax.random.uniform(jax.random.fold_in(own, axis_at), (blocks,), jnp.float32, least / len(cuts), high / len(cuts)))
        level = level * jnp.repeat(draws, extent[axis_at] // blocks).reshape([-1 if axis == axis_at else 1 for axis in range(len(extent))])
    return level


def noise(own_key, dims, width, most, cuts=(), held_as=jnp.bfloat16):
    values = width * jax.random.normal(own_key, dims, jnp.float32)
    if cuts:
        values = values * level_of(own_key, dims, cuts, -0.22, 0.18)
    return jnp.clip(values, -most, most).astype(held_as)


def setup_inputs(seed: int = 0) -> dict:
    arg_keys = jax.random.split(jax.random.key(seed), 5)
    weights = draw_weights(jax.random.fold_in(arg_keys[4], 71), 0)
    hidden = noise(arg_keys[1], (REPLICAS, TOKENS, FF), 1.0, 6.0, ((0, 32), (2, 16)))
    out_grad = noise(arg_keys[2], (REPLICAS, TOKENS, D), 1.0, 6.0, ((0, 32), (1, 16)))
    q_start = noise(arg_keys[3], (REPLICAS, D, R), 1.0, 6.0, ((0, 32),), jnp.float32)
    return {"weights": weights, "hidden": hidden, "out_grad": out_grad, "q_start": q_start}


highest = lax.Precision.HIGHEST

def solve_lower(lower_factor, matrix):
    columns = []
    for k in range(matrix.shape[-1]):
        vector = matrix[..., k]
        for j in range(k):
            vector = vector - lower_factor[..., k, j][..., None] * columns[j]
        columns.append(vector / lower_factor[..., k, k][..., None])
    return jnp.stack(columns, axis=-1)

def make_params(weights, hidden, out_grad, index):
    weight_now = lax.dynamic_index_in_dim(weights, index, 0, keepdims=False)
    hidden_now = lax.dynamic_index_in_dim(hidden, index, 0, keepdims=False)
    grad_now = lax.dynamic_index_in_dim(out_grad, index, 0, keepdims=False)
    gradient = lax.dot_general(hidden_now.astype(jnp.float32), grad_now.astype(jnp.float32), (((0,), (0,)), ((), ())), preferred_element_type=jnp.float32)
    return weight_now.astype(jnp.float32) - 0.5 / math.sqrt(hidden.shape[1]) * gradient

def edge_pair(upper, lower, factor):
    phat = None
    for round_index in range(ROUNDS):
        left_factor = jnp.dot(upper, factor, precision=highest) - jnp.dot(lower, factor, precision=highest)
        gram = jnp.dot(left_factor.T, left_factor, precision=highest)
        phat = solve_lower(jnp.linalg.cholesky(gram), left_factor)
        factor = jnp.dot(upper.T, phat, precision=highest) - jnp.dot(lower.T, phat, precision=highest)
    return (phat, factor)

def reference(weights, hidden, out_grad, q_start):
    count = weights.shape[0]
    first = make_params(weights, hidden, out_grad, jnp.int32(0))
    empty_p = jnp.zeros((weights.shape[1], q_start.shape[2]), jnp.float32)
    empty_q = jnp.zeros((weights.shape[2], q_start.shape[2]), jnp.float32)

    def advance(carry, index):
        current, prev_p, prev_q = carry
        following = make_params(weights, hidden, out_grad, ((index + 1) % count).astype(jnp.int32))
        start_q = lax.dynamic_index_in_dim(q_start, index, 0, keepdims=False)
        phat, factor = edge_pair(current, following, start_q)
        update = current - 0.5 * jnp.dot(phat, factor.T, precision=highest) + 0.5 * jnp.dot(prev_p, prev_q.T, precision=highest)
        return ((following, phat, factor), (update.astype(jnp.bfloat16), phat, factor))
    carry, outputs = lax.scan(advance, (first, empty_p, empty_q), jnp.arange(count, dtype=jnp.int32))
    last_params, last_p, last_q = carry
    updates, phats, factors = outputs
    fixed = last_params - 0.5 * jnp.dot(phats[0], factors[0].T, precision=highest) + 0.5 * jnp.dot(last_p, last_q.T, precision=highest)
    updates = updates.at[0].set(fixed.astype(jnp.bfloat16))
    return (updates, factors)
```

```python
import functools
import math

import jax
import jax.numpy as jnp
from jax import lax
from jax.experimental import pallas as pl
from jax.experimental.pallas import tpu as pltpu
from jax.sharding import PartitionSpec as P

ROUNDS = 2
MESH = pl.DeviceIdType.MESH
F32, BF16 = jnp.float32, jnp.bfloat16

NT = (((1,), (1,)), ((), ()))
NN = (((1,), (0,)), ((), ()))
TN = (((0,), (0,)), ((), ()))


def mm(a, b, dims):
    return lax.dot_general(a, b, dims, preferred_element_type=F32)


def pieces(x):
    high = x.astype(BF16).astype(F32)
    rest = x - high
    mid = rest.astype(BF16).astype(F32)
    low = rest - mid
    return jnp.concatenate([high, mid, low], axis=0).astype(BF16)


def joined(y):
    n = y.shape[0] // 3
    return y[:n] + (y[n : 2 * n] + y[2 * n :])


def edge_row(x, k, first):
    return jnp.where(
        first,
        jnp.broadcast_to(x[k : k + 1], x.shape),
        jnp.broadcast_to(x[4 + k : 5 + k], x.shape),
    )


def eliminate(q, m, others):
    rows = lax.broadcasted_iota(jnp.int32, (8, 1), 0)
    first = rows < 4
    within = rows - jnp.where(first, 0, 4)
    gram = [jnp.sum(m * edge_row(q, k, first), axis=1, keepdims=True) for k in range(4)]
    arrays = [m] + others
    diagonal = jnp.zeros((8, 1), F32)
    for k in range(4):
        pivot = edge_row(gram[k], k, first)
        diagonal = jnp.where(within == k, gram[k], diagonal)
        factor = jnp.where(within > k, gram[k] / pivot, 0.0)
        if k < 3:
            for j in range(k + 1, 4):
                gram[j] = gram[j] - factor * edge_row(gram[j], k, first)
            arrays = [a - factor * edge_row(a, k, first) for a in arrays]
    scale = 1.0 / jnp.sqrt(diagonal)
    return [a * scale for a in arrays]


def kernel(n_blk, n_fsdp, step, w_hbm, h_hbm, g_hbm, q_hbm, new_hbm, edge_ref,
           w, h, g, base, out, g_ref, q_ref, q_left, q_all, p_send, p_recv, m_part, m_recv, m_sum,
           x_send, x_recv, in_sem, out_sem, q_sem, g_sem, p_sem, rs_sem, ag_sem, x_sem):
    b, f = lax.axis_index("blk"), lax.axis_index("fsdp")
    up, down = lax.rem(b + 1, n_blk), lax.rem(b + n_blk - 1, n_blk)
    half = n_fsdp // 2
    mine = lax.rem(f, half)
    start_of_half = f - mine
    rows, width = w.shape
    strip = width // (half // 2)

    def remote(src, dst, sems, at, where):
        return pltpu.make_async_remote_copy(
            src_ref=src, dst_ref=dst, send_sem=sems.at[at], recv_sem=sems.at[at + 1],
            device_id=where, device_id_type=MESH,
        )

    def settle(ref, sem):
        pltpu.make_async_copy(ref, ref, sem).wait()

    load_w = pltpu.make_async_copy(w_hbm, w, in_sem.at[0])
    load_h = pltpu.make_async_copy(h_hbm, h, in_sem.at[1])
    load_g = pltpu.make_async_copy(g_hbm, g_ref, in_sem.at[2])
    load_q = pltpu.make_async_copy(q_hbm, q_ref, in_sem.at[3])
    for load in (load_q, load_g, load_w, load_h):
        load.start()
    others = [(b, lax.rem(f + k, n_fsdp)) for k in range(1, n_fsdp)]
    barrier = pltpu.get_barrier_semaphore()
    for where in others + [(up, f), (down, f)]:
        pl.semaphore_signal(barrier, inc=1, device_id=where, device_id_type=MESH)
    pl.semaphore_wait(barrier, n_fsdp + 1)

    load_q.wait()
    load_g.wait()
    send_q = remote(q_ref, q_left, q_sem, 0, (up, f))
    send_q.start()
    for where in others:
        remote(g_ref, g.at[f], g_sem, 0, where).start()
    g[f] = g_ref[...]
    q_all[0:4] = q_ref[...]
    load_w.wait()
    load_h.wait()
    send_q.wait_recv()
    q_all[4:8] = q_left[...]
    q = q_all[...]

    def gather_g():
        settle(g.at[pl.ds(0, n_fsdp - 1)], g_sem.at[1])

    for r in range(ROUNDS):
        q3 = pieces(q)
        own = joined(mm(q3, w[...], NT))
        if r == 0:
            gather_g()
        tokens = g[...].reshape(n_fsdp * g.shape[1], width)
        own = own - joined(mm(pieces(step * joined(mm(q3, tokens, NT))), h[...], NN))
        p_send[r, 0] = own[0:4]
        p_send[r, 1] = own[4:8]
        to_up = remote(p_send.at[r, 0], p_recv.at[r, 1], p_sem, 4 * r, (up, f))
        to_down = remote(p_send.at[r, 1], p_recv.at[r, 0], p_sem, 4 * r + 2, (down, f))
        to_up.start()
        to_down.start()
        if r == 0:
            for i in range(0, rows, 128):
                base[i : i + 128] = w[i : i + 128].astype(F32) - step * mm(h[:, i : i + 128], tokens, TN)
        to_up.wait_recv()
        to_down.wait_recv()
        p = jnp.concatenate([own[0:4] - p_recv[r, 0], p_recv[r, 1] - own[4:8]], axis=0)
        p3 = pieces(p)
        part = joined(mm(p3, w[...], NN))
        part = part - joined(mm(pieces(step * joined(mm(p3, h[...], NT))), tokens, NN))
        for s in range(half):
            i, j = 4 * (s // (half // 2)), strip * (s % (half // 2))
            m_part[r, s] = part[i : i + 4, j : j + strip]
        for k in range(1, half):
            to = lax.rem(mine + k, half)
            remote(m_part.at[r, to], m_recv.at[r, mine], rs_sem, 2 * r, (b, start_of_half + to)).start()
        m_recv[r, mine] = m_part[r, mine]
        settle(m_recv.at[r, pl.ds(0, half - 1)], rs_sem.at[2 * r + 1])
        total = m_recv[r, 0]
        for s in range(1, half):
            total = total + m_recv[r, s]
        m_sum[r, f] = total
        for where in others:
            remote(m_sum.at[r, f], m_sum.at[r, f], ag_sem, 2 * r, where).start()
        settle(m_sum.at[r, pl.ds(0, n_fsdp - 1)], ag_sem.at[2 * r + 1])
        for s in range(half):
            e, j = s // (half // 2), strip * (s % (half // 2))
            x_send[r, e, :, j : j + strip] = m_sum[r, s] + m_sum[r, half + s]
        to_up = remote(x_send.at[r, 0], x_recv.at[r, 1], x_sem, 4 * r, (up, f))
        to_down = remote(x_send.at[r, 1], x_recv.at[r, 0], x_sem, 4 * r + 2, (down, f))
        to_up.start()
        to_down.start()
        to_up.wait_recv()
        to_down.wait_recv()
        m = jnp.concatenate(
            [x_send[r, 0] - x_recv[r, 0], x_recv[r, 1] - x_send[r, 1]], axis=0
        )
        if r < ROUNDS - 1:
            (q,) = eliminate(q, m, [])
        else:
            q, p = eliminate(q, m, [p])

    edge_ref[...] = q[0:4]
    sign = jnp.where(lax.broadcasted_iota(jnp.int32, (8, 1), 0) < 4, -0.5, 0.5)
    q3, p3 = pieces(q), pieces(sign * p)
    left = jnp.concatenate([p3[0:8], p3[0:8], p3[8:16], p3[0:8], p3[16:24], p3[8:16]], axis=0)
    right = jnp.concatenate([q3[0:8], q3[8:16], q3[0:8], q3[16:24], q3[0:8], q3[8:16]], axis=0)
    saves = []
    for n, i in enumerate(range(0, rows, 128)):
        out[i : i + 128] = (base[i : i + 128] + mm(left[:, i : i + 128], right, TN)).astype(BF16)
        save = pltpu.make_async_copy(out.at[i : i + 128], new_hbm.at[i : i + 128], out_sem.at[n])
        save.start()
        saves.append(save)

    send_q.wait_send()
    settle(g.at[pl.ds(0, n_fsdp - 1)], g_sem.at[0])
    for r in range(ROUNDS):
        settle(p_send.at[r, 0], p_sem.at[4 * r])
        settle(p_send.at[r, 1], p_sem.at[4 * r + 2])
        settle(m_recv.at[r, pl.ds(0, half - 1)], rs_sem.at[2 * r])
        settle(m_sum.at[r, pl.ds(0, n_fsdp - 1)], ag_sem.at[2 * r])
        settle(x_send.at[r, 0], x_sem.at[4 * r])
        settle(x_send.at[r, 1], x_sem.at[4 * r + 2])
    for save in saves:
        save.wait()


def on_device(n_blk, n_fsdp, weights, hidden, out_grad, q_start):
    w, h, g, q = weights[0], hidden[0], out_grad[0], q_start[0].T
    rows, width = w.shape
    tokens = h.shape[0]
    rank = q.shape[0]
    half = n_fsdp // 2
    strip = width // (half // 2)
    dma = pltpu.SemaphoreType.DMA
    vmem = pl.BlockSpec(memory_space=pltpu.VMEM)
    hbm = pl.BlockSpec(memory_space=pl.ANY)
    new, edge = pl.pallas_call(
        functools.partial(kernel, n_blk, n_fsdp, 0.5 / math.sqrt(tokens)),
        out_shape=(
            jax.ShapeDtypeStruct((rows, width), BF16),
            jax.ShapeDtypeStruct((rank, width), F32),
        ),
        in_specs=[hbm, hbm, hbm, hbm],
        out_specs=(hbm, vmem),
        scratch_shapes=[
            pltpu.VMEM((rows, width), BF16),
            pltpu.VMEM((tokens, rows), BF16),
            pltpu.VMEM((n_fsdp, tokens // n_fsdp, width), BF16),
            pltpu.VMEM((rows, width), F32),
            pltpu.VMEM((rows, width), BF16),
            pltpu.VMEM((tokens // n_fsdp, width), BF16),
            pltpu.VMEM((rank, width), F32),
            pltpu.VMEM((rank, width), F32),
            pltpu.VMEM((2 * rank, width), F32),
            pltpu.VMEM((ROUNDS, 2, rank, rows), F32),
            pltpu.VMEM((ROUNDS, 2, rank, rows), F32),
            pltpu.VMEM((ROUNDS, half, rank, strip), F32),
            pltpu.VMEM((ROUNDS, half, rank, strip), F32),
            pltpu.VMEM((ROUNDS, n_fsdp, rank, strip), F32),
            pltpu.VMEM((ROUNDS, 2, rank, width), F32),
            pltpu.VMEM((ROUNDS, 2, rank, width), F32),
            dma((4,)),
            dma((rows // 128,)),
            dma((2,)),
            dma((2,)),
            dma((4 * ROUNDS,)),
            dma((2 * ROUNDS,)),
            dma((2 * ROUNDS,)),
            dma((4 * ROUNDS,)),
        ],
        compiler_params=pltpu.CompilerParams(
            collective_id=0, has_side_effects=True, vmem_limit_bytes=60 << 20
        ),
    )(w, h, g, q)
    return new[None], edge.T[None]


def solution(mesh):
    placed = (
        P("blk", "fsdp", None),
        P("blk", None, "fsdp"),
        P("blk", "fsdp", None),
        P("blk", None, None),
    )
    return jax.shard_map(
        functools.partial(on_device, mesh.shape["blk"], mesh.shape["fsdp"]),
        mesh=mesh,
        in_specs=placed,
        out_specs=(P("blk", "fsdp", None), P("blk", None, None)),
        check_vma=False,
    )
```

```python
import functools
import math

import jax
import jax.numpy as jnp
from jax import lax
from jax.experimental import pallas as pl
from jax.experimental.pallas import tpu as pltpu
from jax.sharding import PartitionSpec as P

ROUNDS = 2
MESH = pl.DeviceIdType.MESH
F32, BF16 = jnp.float32, jnp.bfloat16

NT = (((1,), (1,)), ((), ()))
NN = (((1,), (0,)), ((), ()))
TN = (((0,), (0,)), ((), ()))


def mm(a, b, dims):
    return lax.dot_general(a, b, dims, preferred_element_type=F32)


def pieces(x):
    high = x.astype(BF16).astype(F32)
    rest = x - high
    mid = rest.astype(BF16).astype(F32)
    low = rest - mid
    return jnp.concatenate([high, mid, low], axis=0).astype(BF16)


def joined(y):
    n = y.shape[0] // 3
    return y[:n] + (y[n : 2 * n] + y[2 * n :])


def edge_row(x, k, first):
    return jnp.where(
        first,
        jnp.broadcast_to(x[k : k + 1], x.shape),
        jnp.broadcast_to(x[4 + k : 5 + k], x.shape),
    )


def eliminate(q, m, others):
    rows = lax.broadcasted_iota(jnp.int32, (8, 1), 0)
    first = rows < 4
    within = rows - jnp.where(first, 0, 4)
    gram = [jnp.sum(m * edge_row(q, k, first), axis=1, keepdims=True) for k in range(4)]
    arrays = [m] + others
    diagonal = jnp.zeros((8, 1), F32)
    for k in range(4):
        pivot = edge_row(gram[k], k, first)
        diagonal = jnp.where(within == k, gram[k], diagonal)
        factor = jnp.where(within > k, gram[k] / pivot, 0.0)
        if k < 3:
            for j in range(k + 1, 4):
                gram[j] = gram[j] - factor * edge_row(gram[j], k, first)
            arrays = [a - factor * edge_row(a, k, first) for a in arrays]
    scale = 1.0 / jnp.sqrt(diagonal)
    return [a * scale for a in arrays]


def kernel(n_blk, n_fsdp, step, w_hbm, h_hbm, g_hbm, q_hbm, base, left, right, edge_ref,
           w, h, g, g_ref, q_ref, q_left, q_all, p_send, p_recv, m_part, m_recv, m_sum,
           m_all, in_sem, q_sem, g_sem, p_sem, rs_sem, ag_sem):
    b, f = lax.axis_index("blk"), lax.axis_index("fsdp")
    up, down = lax.rem(b + 1, n_blk), lax.rem(b + n_blk - 1, n_blk)
    half = n_fsdp // 2
    mine = lax.rem(f, half)
    start_of_half = f - mine
    rows, width = w.shape
    strip = width // (half // 2)

    def remote(src, dst, sems, at, where):
        return pltpu.make_async_remote_copy(
            src_ref=src, dst_ref=dst, send_sem=sems.at[at], recv_sem=sems.at[at + 1],
            device_id=where, device_id_type=MESH,
        )

    def settle(ref, sem):
        pltpu.make_async_copy(ref, ref, sem).wait()

    load_w = pltpu.make_async_copy(w_hbm, w, in_sem.at[0])
    load_h = pltpu.make_async_copy(h_hbm, h, in_sem.at[1])
    load_g = pltpu.make_async_copy(g_hbm, g_ref, in_sem.at[2])
    load_q = pltpu.make_async_copy(q_hbm, q_ref, in_sem.at[3])
    for load in (load_q, load_g, load_w, load_h):
        load.start()
    others = [(b, lax.rem(f + k, n_fsdp)) for k in range(1, n_fsdp)]
    barrier = pltpu.get_barrier_semaphore()
    beside = [(there, start_of_half + s) for there in (up, down) for s in range(half)]
    for where in others + beside:
        pl.semaphore_signal(barrier, inc=1, device_id=where, device_id_type=MESH)
    pl.semaphore_wait(barrier, len(others) + len(beside))

    load_q.wait()
    load_g.wait()
    send_q = remote(q_ref, q_left, q_sem, 0, (up, f))
    send_q.start()
    for where in others:
        remote(g_ref, g.at[f], g_sem, 0, where).start()
    g[f] = g_ref[...]
    q_all[0:4] = q_ref[...]
    load_w.wait()
    load_h.wait()
    send_q.wait_recv()
    q_all[4:8] = q_left[...]
    q = q_all[...]

    def gather_g():
        settle(g.at[pl.ds(0, n_fsdp - 1)], g_sem.at[1])

    for r in range(ROUNDS):
        q3 = pieces(q)
        own = joined(mm(q3, w[...], NT))
        if r == 0:
            gather_g()
        tokens = g[...].reshape(n_fsdp * g.shape[1], width)
        own = own - joined(mm(pieces(step * joined(mm(q3, tokens, NT))), h[...], NN))
        p_send[r, 0] = own[0:4]
        p_send[r, 1] = own[4:8]
        to_up = remote(p_send.at[r, 0], p_recv.at[r, 1], p_sem, 4 * r, (up, f))
        to_down = remote(p_send.at[r, 1], p_recv.at[r, 0], p_sem, 4 * r + 2, (down, f))
        to_up.start()
        to_down.start()
        if r == 0:
            for i in range(0, rows, 128):
                base[i : i + 128] = w[i : i + 128].astype(F32) - step * mm(h[:, i : i + 128], tokens, TN)
        to_up.wait_recv()
        to_down.wait_recv()
        p = jnp.concatenate([own[0:4] - p_recv[r, 0], p_recv[r, 1] - own[4:8]], axis=0)
        p3 = pieces(p)
        part = joined(mm(p3, w[...], NN))
        part = part - joined(mm(pieces(step * joined(mm(p3, h[...], NT))), tokens, NN))
        for s in range(half):
            i, j = 4 * (s // (half // 2)), strip * (s % (half // 2))
            m_part[r, s] = part[i : i + 4, j : j + strip]
        for s in range(half // 2):
            remote(m_part.at[r, s], m_recv.at[r, half + mine], rs_sem, 2 * r, (up, start_of_half + half // 2 + s)).start()
            remote(m_part.at[r, half // 2 + s], m_recv.at[r, half + mine], rs_sem, 2 * r, (down, start_of_half + s)).start()
        for k in range(1, half):
            to = lax.rem(mine + k, half)
            remote(m_part.at[r, to], m_recv.at[r, mine], rs_sem, 2 * r, (b, start_of_half + to)).start()
        m_recv[r, mine] = m_part[r, mine]
        settle(m_recv.at[r, pl.ds(0, 2 * half - 1)], rs_sem.at[2 * r + 1])
        total = m_recv[r, 0] - m_recv[r, half]
        for s in range(1, half):
            total = total + (m_recv[r, s] - m_recv[r, half + s])
        m_sum[r, f] = jnp.where(mine < half // 2, 1.0, -1.0) * total
        for where in others:
            remote(m_sum.at[r, f], m_sum.at[r, f], ag_sem, 2 * r, where).start()
        settle(m_sum.at[r, pl.ds(0, n_fsdp - 1)], ag_sem.at[2 * r + 1])
        for s in range(half):
            i, j = 4 * (s // (half // 2)), strip * (s % (half // 2))
            m_all[i : i + 4, j : j + strip] = m_sum[r, s] + m_sum[r, half + s]
        m = m_all[...]
        if r < ROUNDS - 1:
            (q,) = eliminate(q, m, [])
        else:
            q, p = eliminate(q, m, [p])

    edge_ref[...] = q[0:4]
    sign = jnp.where(lax.broadcasted_iota(jnp.int32, (8, 1), 0) < 4, -0.5, 0.5)
    q3, p3 = pieces(q), pieces(sign * p)
    left[...] = jnp.concatenate([p3[0:8], p3[0:8], p3[8:16], p3[0:8], p3[16:24], p3[8:16]], axis=0)
    right[...] = jnp.concatenate([q3[0:8], q3[8:16], q3[0:8], q3[16:24], q3[0:8], q3[8:16]], axis=0)

    send_q.wait_send()
    settle(g.at[pl.ds(0, n_fsdp - 1)], g_sem.at[0])
    for r in range(ROUNDS):
        settle(p_send.at[r, 0], p_sem.at[4 * r])
        settle(p_send.at[r, 1], p_sem.at[4 * r + 2])
        settle(m_recv.at[r, pl.ds(0, 2 * half - 1)], rs_sem.at[2 * r])
        settle(m_sum.at[r, pl.ds(0, n_fsdp - 1)], ag_sem.at[2 * r])


def write_kernel(base, left, right, edge, new_hbm, edge_hbm, new, sem):
    saves = [pltpu.make_async_copy(edge, edge_hbm, sem.at[0])]
    saves[0].start()
    for n, i in enumerate(range(0, base.shape[0], 128)):
        at = pl.ds(i, 128)
        new[at] = (base[at] + mm(left[:, at], right[...], TN)).astype(BF16)
        saves.append(pltpu.make_async_copy(new.at[at], new_hbm.at[at], sem.at[1 + n]))
        saves[-1].start()
    for save in saves:
        save.wait()


def on_device(n_blk, n_fsdp, weights, hidden, out_grad, q_start):
    w, h, g, q = weights[0], hidden[0], out_grad[0], q_start[0].T
    rows, width = w.shape
    tokens = h.shape[0]
    rank = q.shape[0]
    half = n_fsdp // 2
    strip = width // (half // 2)
    dma = pltpu.SemaphoreType.DMA
    vmem = pl.BlockSpec(memory_space=pltpu.VMEM)
    hbm = pl.BlockSpec(memory_space=pl.ANY)
    parts = pl.pallas_call(
        functools.partial(kernel, n_blk, n_fsdp, 0.5 / math.sqrt(tokens)),
        out_shape=(
            pltpu.VMEM((rows, width), F32),
            pltpu.VMEM((12 * rank, rows), BF16),
            pltpu.VMEM((12 * rank, width), BF16),
            pltpu.VMEM((rank, width), F32),
        ),
        in_specs=[hbm, hbm, hbm, hbm],
        out_specs=(vmem, vmem, vmem, vmem),
        scratch_shapes=[
            pltpu.VMEM((rows, width), BF16),
            pltpu.VMEM((tokens, rows), BF16),
            pltpu.VMEM((n_fsdp, tokens // n_fsdp, width), BF16),
            pltpu.VMEM((tokens // n_fsdp, width), BF16),
            pltpu.VMEM((rank, width), F32),
            pltpu.VMEM((rank, width), F32),
            pltpu.VMEM((2 * rank, width), F32),
            pltpu.VMEM((ROUNDS, 2, rank, rows), F32),
            pltpu.VMEM((ROUNDS, 2, rank, rows), F32),
            pltpu.VMEM((ROUNDS, half, rank, strip), F32),
            pltpu.VMEM((ROUNDS, 2 * half, rank, strip), F32),
            pltpu.VMEM((ROUNDS, n_fsdp, rank, strip), F32),
            pltpu.VMEM((2 * rank, width), F32),
            dma((4,)),
            dma((2,)),
            dma((2,)),
            dma((4 * ROUNDS,)),
            dma((2 * ROUNDS,)),
            dma((2 * ROUNDS,)),
        ],
        compiler_params=pltpu.CompilerParams(
            collective_id=0, has_side_effects=True, vmem_limit_bytes=40 << 20
        ),
    )(*(pltpu.with_memory_space_constraint(x, pltpu.HBM) for x in (w, h, g, q)))
    new, edge = pl.pallas_call(
        write_kernel,
        out_shape=(
            jax.ShapeDtypeStruct((rows, width), BF16),
            jax.ShapeDtypeStruct((rank, width), F32),
        ),
        in_specs=[vmem] * 4,
        out_specs=(hbm, hbm),
        scratch_shapes=[pltpu.VMEM((rows, width), BF16), dma((rows // 128 + 1,))],
        compiler_params=pltpu.CompilerParams(vmem_limit_bytes=16 << 20),
    )(*(pltpu.with_memory_space_constraint(x, pltpu.VMEM) for x in parts))
    return new[None], edge.T[None]


def solution(mesh):
    placed = (
        P("blk", "fsdp", None),
        P("blk", None, "fsdp"),
        P("blk", "fsdp", None),
        P("blk", None, None),
    )
    return jax.shard_map(
        functools.partial(on_device, mesh.shape["blk"], mesh.shape["fsdp"]),
        mesh=mesh,
        in_specs=placed,
        out_specs=(P("blk", "fsdp", None), P("blk", None, None)),
        check_vma=False,
    )
```

```python
import functools
import math

import jax
import jax.numpy as jnp
from jax import lax
from jax.experimental import pallas as pl
from jax.experimental.pallas import tpu as pltpu
from jax.sharding import PartitionSpec as P

ROUNDS = 2
MESH = pl.DeviceIdType.MESH
F32, BF16 = jnp.float32, jnp.bfloat16

NT = (((1,), (1,)), ((), ()))
NN = (((1,), (0,)), ((), ()))
TN = (((0,), (0,)), ((), ()))


def mm(a, b, dims):
    return lax.dot_general(a, b, dims, preferred_element_type=F32)


def pieces(x):
    high = x.astype(BF16).astype(F32)
    rest = x - high
    mid = rest.astype(BF16).astype(F32)
    low = rest - mid
    return jnp.concatenate([high, mid, low], axis=0).astype(BF16)


def joined(y):
    n = y.shape[0] // 3
    return y[:n] + (y[n : 2 * n] + y[2 * n :])


def edge_row(x, k, first):
    return jnp.where(
        first,
        jnp.broadcast_to(x[k : k + 1], x.shape),
        jnp.broadcast_to(x[4 + k : 5 + k], x.shape),
    )


def eliminate(q, m, others):
    rows = lax.broadcasted_iota(jnp.int32, (8, 1), 0)
    first = rows < 4
    within = rows - jnp.where(first, 0, 4)
    gram = [jnp.sum(m * edge_row(q, k, first), axis=1, keepdims=True) for k in range(4)]
    arrays = [m] + others
    diagonal = jnp.zeros((8, 1), F32)
    for k in range(4):
        pivot = edge_row(gram[k], k, first)
        diagonal = jnp.where(within == k, gram[k], diagonal)
        factor = jnp.where(within > k, gram[k] / pivot, 0.0)
        if k < 3:
            for j in range(k + 1, 4):
                gram[j] = gram[j] - factor * edge_row(gram[j], k, first)
            arrays = [a - factor * edge_row(a, k, first) for a in arrays]
    scale = 1.0 / jnp.sqrt(diagonal)
    return [a * scale for a in arrays]


def kernel(n_blk, n_fsdp, step, w_hbm, h_hbm, g_hbm, q_hbm, base, left, right, edge_ref,
           w, h, g, g_ref, g_pad, gq, q_ref, q_left, q_all, p_send, p_recv, m_part, m_recv, m_sum,
           m_all, in_sem, q_sem, gq_sem, g_sem, p_sem, rs_sem, ag_sem):
    b, f = lax.axis_index("blk"), lax.axis_index("fsdp")
    up, down = lax.rem(b + 1, n_blk), lax.rem(b + n_blk - 1, n_blk)
    half = n_fsdp // 2
    mine = lax.rem(f, half)
    start_of_half = f - mine
    rows, width = w.shape
    strip = width // (half // 2)

    def remote(src, dst, sems, at, where):
        return pltpu.make_async_remote_copy(
            src_ref=src, dst_ref=dst, send_sem=sems.at[at], recv_sem=sems.at[at + 1],
            device_id=where, device_id_type=MESH,
        )

    def settle(ref, sem):
        pltpu.make_async_copy(ref, ref, sem).wait()

    load_w = pltpu.make_async_copy(w_hbm, w, in_sem.at[0])
    load_h = pltpu.make_async_copy(h_hbm, h, in_sem.at[1])
    load_g = pltpu.make_async_copy(g_hbm, g_ref, in_sem.at[2])
    load_q = pltpu.make_async_copy(q_hbm, q_ref, in_sem.at[3])
    for load in (load_q, load_g, load_w, load_h):
        load.start()
    others = [(b, lax.rem(f + k, n_fsdp)) for k in range(1, n_fsdp)]
    barrier = pltpu.get_barrier_semaphore()
    beside = [(there, start_of_half + s) for there in (up, down) for s in range(half)]
    for where in others + beside:
        pl.semaphore_signal(barrier, inc=1, device_id=where, device_id_type=MESH)
    pl.semaphore_wait(barrier, len(others) + len(beside))

    load_q.wait()
    load_g.wait()
    send_q = remote(q_ref, q_left, q_sem, 0, (up, f))
    send_q.start()
    line = [lax.rem(f + 2 * k, n_fsdp) for k in range(1, half)]
    mate = f + 1 - 2 * lax.rem(f, 2)
    for there in line:
        remote(g_ref, g.at[f], g_sem, 0, (b, there)).start()
    g[f] = g_ref[...]
    q_all[0:4] = q_ref[...]
    block = g_ref.shape[0]
    per_tile = g_pad.shape[0] // block
    g_pad[...] = jnp.zeros_like(g_pad)
    g_pad[pl.ds(pl.multiple_of(block * lax.rem(f, per_tile), block), block)] = g_ref[...]
    send_q.wait_recv()
    q_all[4:8] = q_left[...]
    q = q_all[...]
    gq[f] = joined(mm(pieces(q), g_pad[...], NT))
    for where in others:
        remote(gq.at[f], gq.at[f], gq_sem, 0, where).start()
    load_w.wait()
    load_h.wait()
    tokens = None

    for r in range(ROUNDS):
        q3 = pieces(q)
        own = joined(mm(q3, w[...], NT))
        if r == 0:
            settle(gq.at[pl.ds(0, n_fsdp - 1)], gq_sem.at[1])
            seen = jnp.concatenate(
                [sum(gq[i + k] for k in range(per_tile)) for i in range(0, n_fsdp, per_tile)], axis=1
            )
        else:
            seen = joined(mm(q3, tokens, NT))
        own = own - joined(mm(pieces(step * seen), h[...], NN))
        p_send[r, 0] = own[0:4]
        p_send[r, 1] = own[4:8]
        to_up = remote(p_send.at[r, 0], p_recv.at[r, 1], p_sem, 4 * r, (up, f))
        to_down = remote(p_send.at[r, 1], p_recv.at[r, 0], p_sem, 4 * r + 2, (down, f))
        to_up.start()
        to_down.start()
        if r == 0:
            settle(g.at[pl.ds(0, half - 1)], g_sem.at[1])
            for there in [f] + line:
                remote(g.at[there], g.at[there], g_sem, 2, (b, mate)).start()
        to_up.wait_recv()
        to_down.wait_recv()
        p = jnp.concatenate([own[0:4] - p_recv[r, 0], p_recv[r, 1] - own[4:8]], axis=0)
        p3 = pieces(p)
        part = joined(mm(p3, w[...], NN))
        if r == 0:
            settle(g.at[pl.ds(0, half)], g_sem.at[3])
            tokens = g[...].reshape(n_fsdp * block, width)
        part = part - joined(mm(pieces(step * joined(mm(p3, h[...], NT))), tokens, NN))
        for s in range(half):
            i, j = 4 * (s // (half // 2)), strip * (s % (half // 2))
            m_part[r, s] = part[i : i + 4, j : j + strip]
        for s in range(half // 2):
            remote(m_part.at[r, s], m_recv.at[r, half + mine], rs_sem, 2 * r, (up, start_of_half + half // 2 + s)).start()
            remote(m_part.at[r, half // 2 + s], m_recv.at[r, half + mine], rs_sem, 2 * r, (down, start_of_half + s)).start()
        for k in range(1, half):
            to = lax.rem(mine + k, half)
            remote(m_part.at[r, to], m_recv.at[r, mine], rs_sem, 2 * r, (b, start_of_half + to)).start()
        m_recv[r, mine] = m_part[r, mine]
        if r == 0:
            for i in range(0, rows, 128):
                base[i : i + 128] = w[i : i + 128].astype(F32) - step * mm(h[:, i : i + 128], tokens, TN)
        settle(m_recv.at[r, pl.ds(0, 2 * half - 1)], rs_sem.at[2 * r + 1])
        total = m_recv[r, 0] - m_recv[r, half]
        for s in range(1, half):
            total = total + (m_recv[r, s] - m_recv[r, half + s])
        m_sum[r, f] = jnp.where(mine < half // 2, 1.0, -1.0) * total
        for where in others:
            remote(m_sum.at[r, f], m_sum.at[r, f], ag_sem, 2 * r, where).start()
        settle(m_sum.at[r, pl.ds(0, n_fsdp - 1)], ag_sem.at[2 * r + 1])
        for s in range(half):
            i, j = 4 * (s // (half // 2)), strip * (s % (half // 2))
            m_all[i : i + 4, j : j + strip] = m_sum[r, s] + m_sum[r, half + s]
        m = m_all[...]
        if r < ROUNDS - 1:
            (q,) = eliminate(q, m, [])
        else:
            q, p = eliminate(q, m, [p])

    edge_ref[...] = q[0:4]
    sign = jnp.where(lax.broadcasted_iota(jnp.int32, (8, 1), 0) < 4, -0.5, 0.5)
    q3, p3 = pieces(q), pieces(sign * p)
    left[...] = jnp.concatenate([p3[0:8], p3[0:8], p3[8:16], p3[0:8], p3[16:24], p3[8:16]], axis=0)
    right[...] = jnp.concatenate([q3[0:8], q3[8:16], q3[0:8], q3[16:24], q3[0:8], q3[8:16]], axis=0)

    send_q.wait_send()
    settle(gq.at[pl.ds(0, n_fsdp - 1)], gq_sem.at[0])
    settle(g.at[pl.ds(0, half - 1)], g_sem.at[0])
    settle(g.at[pl.ds(0, half)], g_sem.at[2])
    for r in range(ROUNDS):
        settle(p_send.at[r, 0], p_sem.at[4 * r])
        settle(p_send.at[r, 1], p_sem.at[4 * r + 2])
        settle(m_recv.at[r, pl.ds(0, 2 * half - 1)], rs_sem.at[2 * r])
        settle(m_sum.at[r, pl.ds(0, n_fsdp - 1)], ag_sem.at[2 * r])


def write_kernel(base, left, right, edge, new_hbm, edge_hbm, new, sem):
    saves = [pltpu.make_async_copy(edge, edge_hbm, sem.at[0])]
    saves[0].start()
    for n, i in enumerate(range(0, base.shape[0], 128)):
        at = pl.ds(i, 128)
        new[at] = (base[at] + mm(left[:, at], right[...], TN)).astype(BF16)
        saves.append(pltpu.make_async_copy(new.at[at], new_hbm.at[at], sem.at[1 + n]))
        saves[-1].start()
    for save in saves:
        save.wait()


def on_device(n_blk, n_fsdp, weights, hidden, out_grad, q_start):
    w, h, g, q = weights[0], hidden[0], out_grad[0], q_start[0].T
    rows, width = w.shape
    tokens = h.shape[0]
    rank = q.shape[0]
    half = n_fsdp // 2
    strip = width // (half // 2)
    dma = pltpu.SemaphoreType.DMA
    vmem = pl.BlockSpec(memory_space=pltpu.VMEM)
    hbm = pl.BlockSpec(memory_space=pl.ANY)
    parts = pl.pallas_call(
        functools.partial(kernel, n_blk, n_fsdp, 0.5 / math.sqrt(tokens)),
        out_shape=(
            pltpu.VMEM((rows, width), F32),
            pltpu.VMEM((12 * rank, rows), BF16),
            pltpu.VMEM((12 * rank, width), BF16),
            pltpu.VMEM((rank, width), F32),
        ),
        in_specs=[hbm, hbm, hbm, hbm],
        out_specs=(vmem, vmem, vmem, vmem),
        scratch_shapes=[
            pltpu.VMEM((rows, width), BF16),
            pltpu.VMEM((tokens, rows), BF16),
            pltpu.VMEM((n_fsdp, tokens // n_fsdp, width), BF16),
            pltpu.VMEM((tokens // n_fsdp, width), BF16),
            pltpu.VMEM((128, width), BF16),
            pltpu.VMEM((n_fsdp, 2 * rank, 128), F32),
            pltpu.VMEM((rank, width), F32),
            pltpu.VMEM((rank, width), F32),
            pltpu.VMEM((2 * rank, width), F32),
            pltpu.VMEM((ROUNDS, 2, rank, rows), F32),
            pltpu.VMEM((ROUNDS, 2, rank, rows), F32),
            pltpu.VMEM((ROUNDS, half, rank, strip), F32),
            pltpu.VMEM((ROUNDS, 2 * half, rank, strip), F32),
            pltpu.VMEM((ROUNDS, n_fsdp, rank, strip), F32),
            pltpu.VMEM((2 * rank, width), F32),
            dma((4,)),
            dma((2,)),
            dma((2,)),
            dma((4,)),
            dma((4 * ROUNDS,)),
            dma((2 * ROUNDS,)),
            dma((2 * ROUNDS,)),
        ],
        compiler_params=pltpu.CompilerParams(
            collective_id=0, has_side_effects=True, vmem_limit_bytes=40 << 20
        ),
    )(*(pltpu.with_memory_space_constraint(x, pltpu.HBM) for x in (w, h, g, q)))
    new, edge = pl.pallas_call(
        write_kernel,
        out_shape=(
            jax.ShapeDtypeStruct((rows, width), BF16),
            jax.ShapeDtypeStruct((rank, width), F32),
        ),
        in_specs=[vmem] * 4,
        out_specs=(hbm, hbm),
        scratch_shapes=[pltpu.VMEM((rows, width), BF16), dma((rows // 128 + 1,))],
        compiler_params=pltpu.CompilerParams(vmem_limit_bytes=16 << 20),
    )(*(pltpu.with_memory_space_constraint(x, pltpu.VMEM) for x in parts))
    return new[None], edge.T[None]


def solution(mesh):
    placed = (
        P("blk", "fsdp", None),
        P("blk", None, "fsdp"),
        P("blk", "fsdp", None),
        P("blk", None, None),
    )
    return jax.shard_map(
        functools.partial(on_device, mesh.shape["blk"], mesh.shape["fsdp"]),
        mesh=mesh,
        in_specs=placed,
        out_specs=(P("blk", "fsdp", None), P("blk", None, None)),
        check_vma=False,
    )
```

```python
import functools
import math

import jax
import jax.numpy as jnp
from jax import lax
from jax.experimental import pallas as pl
from jax.experimental.pallas import tpu as pltpu
from jax.sharding import PartitionSpec as P

ROUNDS = 2
MESH = pl.DeviceIdType.MESH
F32, BF16 = jnp.float32, jnp.bfloat16

NT = (((1,), (1,)), ((), ()))
NN = (((1,), (0,)), ((), ()))
TN = (((0,), (0,)), ((), ()))


def mm(a, b, dims):
    return lax.dot_general(a, b, dims, preferred_element_type=F32)


def pieces(x):
    high = x.astype(BF16).astype(F32)
    rest = x - high
    mid = rest.astype(BF16).astype(F32)
    low = rest - mid
    return jnp.concatenate([high, mid, low], axis=0).astype(BF16)


def joined(y):
    n = y.shape[0] // 3
    return y[:n] + (y[n : 2 * n] + y[2 * n :])


def edge_row(x, k, first):
    return jnp.where(
        first,
        jnp.broadcast_to(x[k : k + 1], x.shape),
        jnp.broadcast_to(x[4 + k : 5 + k], x.shape),
    )


def eliminate(q, m, others):
    rows = lax.broadcasted_iota(jnp.int32, (8, 1), 0)
    first = rows < 4
    within = rows - jnp.where(first, 0, 4)
    gram = [jnp.sum(m * edge_row(q, k, first), axis=1, keepdims=True) for k in range(4)]
    arrays = [m] + others
    diagonal = jnp.zeros((8, 1), F32)
    for k in range(4):
        pivot = edge_row(gram[k], k, first)
        diagonal = jnp.where(within == k, gram[k], diagonal)
        factor = jnp.where(within > k, gram[k] / pivot, 0.0)
        if k < 3:
            for j in range(k + 1, 4):
                gram[j] = gram[j] - factor * edge_row(gram[j], k, first)
            arrays = [a - factor * edge_row(a, k, first) for a in arrays]
    scale = 1.0 / jnp.sqrt(diagonal)
    return [a * scale for a in arrays]


def kernel(n_blk, n_fsdp, step, w_hbm, h_hbm, g_hbm, q_hbm, base, left, right, edge_ref,
           w, h, g, g_ref, g_pad, gq, q_ref, q_left, q_all, p_send, p_recv, m_part, m_recv, m_sum,
           m_all, in_sem, q_sem, gq_sem, g_sem, p_sem, rs_sem, ag_sem):
    b, f = lax.axis_index("blk"), lax.axis_index("fsdp")
    up, down = lax.rem(b + 1, n_blk), lax.rem(b + n_blk - 1, n_blk)
    half = n_fsdp // 2
    mine = lax.rem(f, half)
    start_of_half = f - mine
    rows, width = w.shape
    strip = width // (half // 2)

    def remote(src, dst, sems, at, where):
        return pltpu.make_async_remote_copy(
            src_ref=src, dst_ref=dst, send_sem=sems.at[at], recv_sem=sems.at[at + 1],
            device_id=where, device_id_type=MESH,
        )

    def settle(ref, sem):
        pltpu.make_async_copy(ref, ref, sem).wait()

    load_w = pltpu.make_async_copy(w_hbm, w, in_sem.at[0])
    load_h = pltpu.make_async_copy(h_hbm, h, in_sem.at[1])
    load_g = pltpu.make_async_copy(g_hbm, g_ref, in_sem.at[2])
    load_q = pltpu.make_async_copy(q_hbm, q_ref, in_sem.at[3])
    for load in (load_q, load_g, load_w, load_h):
        load.start()
    others = [(b, lax.rem(f + k, n_fsdp)) for k in sorted(range(1, n_fsdp), key=lambda k: abs(k - half))]
    barrier = pltpu.get_barrier_semaphore()
    odd = lax.rem(mine, 2)
    mainly, also = jnp.where(odd == 1, up, down), jnp.where(odd == 1, down, up)
    beside = [(mainly, start_of_half + s) for s in range(half)]
    beside += [(also, start_of_half + 2 * s + odd) for s in range(half // 2)]
    for where in others + beside:
        pl.semaphore_signal(barrier, inc=1, device_id=where, device_id_type=MESH)
    pl.semaphore_wait(barrier, len(others) + len(beside))

    load_q.wait()
    load_g.wait()
    send_q = remote(q_ref, q_left, q_sem, 0, (up, f))
    send_q.start()
    mate = f + 1 - 2 * lax.rem(f, 2)

    def along_z(k):
        return lax.rem(f + 2 * k + n_fsdp, n_fsdp)

    def pass_to_mate(owners):
        for there in owners:
            remote(g.at[there], g.at[there], g_sem, 4, (b, mate)).start()

    near = [along_z(k) for k in (1, -1, 2, -2)]
    far = [along_z(k) for k in (3, -3, 4)]
    for there in near:
        remote(g_ref, g.at[f], g_sem, 0, (b, there)).start()
    remote(g_ref, g.at[f], g_sem, 4, (b, mate)).start()
    g[f] = g_ref[...]
    q_all[0:4] = q_ref[...]
    block = g_ref.shape[0]
    per_tile = g_pad.shape[0] // block
    g_pad[...] = jnp.zeros_like(g_pad)
    g_pad[pl.ds(pl.multiple_of(block * lax.rem(f, per_tile), block), block)] = g_ref[...]
    send_q.wait_recv()
    q_all[4:8] = q_left[...]
    q = q_all[...]
    gq[f] = joined(mm(pieces(q), g_pad[...], NT))
    for where in others:
        remote(gq.at[f], gq.at[f], gq_sem, 0, where).start()
    settle(g.at[pl.ds(0, len(near))], g_sem.at[1])
    for held, to in ((2, -1), (-2, 1), (2, -2)):
        held = along_z(held)
        remote(g.at[held], g.at[held], g_sem, 2, (b, along_z(to))).start()
    pass_to_mate(near)
    load_w.wait()
    load_h.wait()
    tokens = None

    for r in range(ROUNDS):
        q3 = pieces(q)
        if r == 0:
            own = joined(mm(q3, w[...], NT))
            settle(gq.at[pl.ds(0, n_fsdp - 1)], gq_sem.at[1])
            seen = jnp.concatenate(
                [sum(gq[i + k] for k in range(per_tile)) for i in range(0, n_fsdp, per_tile)], axis=1
            )
        else:
            seen = joined(mm(q3, tokens, NT))
            own = joined(mm(q3, w[...], NT))
        own = own - joined(mm(pieces(step * seen), h[...], NN))
        p_send[r, 0] = own[0:4]
        p_send[r, 1] = own[4:8]
        to_up = remote(p_send.at[r, 0], p_recv.at[r, 1], p_sem, 4 * r, (up, f))
        to_down = remote(p_send.at[r, 1], p_recv.at[r, 0], p_sem, 4 * r + 2, (down, f))
        to_up.start()
        to_down.start()
        if r == 0:
            settle(g.at[pl.ds(0, len(far))], g_sem.at[3])
            pass_to_mate(far)
        to_up.wait_recv()
        to_down.wait_recv()
        p = jnp.concatenate([own[0:4] - p_recv[r, 0], p_recv[r, 1] - own[4:8]], axis=0)
        p3 = pieces(p)
        seen = joined(mm(p3, h[...], NT))
        part = joined(mm(p3, w[...], NN))
        if r == 0:
            settle(g.at[pl.ds(0, half)], g_sem.at[5])
            tokens = g[...].reshape(n_fsdp * block, width)
        part = part - joined(mm(pieces(step * seen), tokens, NN))
        for s in range(half):
            i, j = 4 - 4 * (s % 2), strip * (s // 2)
            m_part[r, s] = part[i : i + 4, j : j + strip]
        for s in range(half // 2):
            above, below = 2 * s + 1, 2 * s
            remote(m_part.at[r, above], m_recv.at[r, half + mine], rs_sem, 2 * r, (up, start_of_half + below)).start()
            remote(m_part.at[r, below], m_recv.at[r, half + mine], rs_sem, 2 * r, (down, start_of_half + above)).start()
        for k in range(1, half):
            to = lax.rem(mine + k, half)
            remote(m_part.at[r, to], m_recv.at[r, mine], rs_sem, 2 * r, (b, start_of_half + to)).start()
        m_recv[r, mine] = m_part[r, mine]
        if r == 0:
            for i in range(0, rows, 128):
                base[i : i + 128] = w[i : i + 128].astype(F32) - step * mm(h[:, i : i + 128], tokens, TN)
        settle(m_recv.at[r, pl.ds(0, 2 * half - 1)], rs_sem.at[2 * r + 1])
        total = m_recv[r, 0] - m_recv[r, half]
        for s in range(1, half):
            total = total + (m_recv[r, s] - m_recv[r, half + s])
        m_sum[r, f] = jnp.where(odd == 1, 1.0, -1.0) * total
        for where in others:
            remote(m_sum.at[r, f], m_sum.at[r, f], ag_sem, 2 * r, where).start()
        settle(m_sum.at[r, pl.ds(0, n_fsdp - 1)], ag_sem.at[2 * r + 1])
        for s in range(half):
            i, j = 4 - 4 * (s % 2), strip * (s // 2)
            m_all[i : i + 4, j : j + strip] = m_sum[r, s] + m_sum[r, half + s]
        m = m_all[...]
        if r < ROUNDS - 1:
            (q,) = eliminate(q, m, [])
        else:
            q, p = eliminate(q, m, [p])

    edge_ref[...] = q[0:4]
    sign = jnp.where(lax.broadcasted_iota(jnp.int32, (8, 1), 0) < 4, -0.5, 0.5)
    q3, p3 = pieces(q), pieces(sign * p)
    left[...] = jnp.concatenate([p3[0:8], p3[0:8], p3[8:16], p3[0:8], p3[16:24], p3[8:16]], axis=0)
    right[...] = jnp.concatenate([q3[0:8], q3[8:16], q3[0:8], q3[16:24], q3[0:8], q3[8:16]], axis=0)

    send_q.wait_send()
    settle(gq.at[pl.ds(0, n_fsdp - 1)], gq_sem.at[0])
    settle(g.at[pl.ds(0, len(near))], g_sem.at[0])
    settle(g.at[pl.ds(0, len(far))], g_sem.at[2])
    settle(g.at[pl.ds(0, half)], g_sem.at[4])
    for r in range(ROUNDS):
        settle(p_send.at[r, 0], p_sem.at[4 * r])
        settle(p_send.at[r, 1], p_sem.at[4 * r + 2])
        settle(m_recv.at[r, pl.ds(0, 2 * half - 1)], rs_sem.at[2 * r])
        settle(m_sum.at[r, pl.ds(0, n_fsdp - 1)], ag_sem.at[2 * r])


def write_kernel(base, left, right, edge, new_hbm, edge_hbm, new, sem):
    saves = [pltpu.make_async_copy(edge, edge_hbm, sem.at[0])]
    saves[0].start()
    for n, i in enumerate(range(0, base.shape[0], 128)):
        at = pl.ds(i, 128)
        new[at] = (base[at] + mm(left[:, at], right[...], TN)).astype(BF16)
        saves.append(pltpu.make_async_copy(new.at[at], new_hbm.at[at], sem.at[1 + n]))
        saves[-1].start()
    for save in saves:
        save.wait()


def on_device(n_blk, n_fsdp, weights, hidden, out_grad, q_start):
    w, h, g, q = weights[0], hidden[0], out_grad[0], q_start[0].T
    rows, width = w.shape
    tokens = h.shape[0]
    rank = q.shape[0]
    half = n_fsdp // 2
    strip = width // (half // 2)
    dma = pltpu.SemaphoreType.DMA
    vmem = pl.BlockSpec(memory_space=pltpu.VMEM)
    hbm = pl.BlockSpec(memory_space=pl.ANY)
    parts = pl.pallas_call(
        functools.partial(kernel, n_blk, n_fsdp, 0.5 / math.sqrt(tokens)),
        out_shape=(
            pltpu.VMEM((rows, width), F32),
            pltpu.VMEM((12 * rank, rows), BF16),
            pltpu.VMEM((12 * rank, width), BF16),
            pltpu.VMEM((rank, width), F32),
        ),
        in_specs=[hbm, hbm, hbm, hbm],
        out_specs=(vmem, vmem, vmem, vmem),
        scratch_shapes=[
            pltpu.VMEM((rows, width), BF16),
            pltpu.VMEM((tokens, rows), BF16),
            pltpu.VMEM((n_fsdp, tokens // n_fsdp, width), BF16),
            pltpu.VMEM((tokens // n_fsdp, width), BF16),
            pltpu.VMEM((128, width), BF16),
            pltpu.VMEM((n_fsdp, 2 * rank, 128), F32),
            pltpu.VMEM((rank, width), F32),
            pltpu.VMEM((rank, width), F32),
            pltpu.VMEM((2 * rank, width), F32),
            pltpu.VMEM((ROUNDS, 2, rank, rows), F32),
            pltpu.VMEM((ROUNDS, 2, rank, rows), F32),
            pltpu.VMEM((ROUNDS, half, rank, strip), F32),
            pltpu.VMEM((ROUNDS, 2 * half, rank, strip), F32),
            pltpu.VMEM((ROUNDS, n_fsdp, rank, strip), F32),
            pltpu.VMEM((2 * rank, width), F32),
            dma((4,)),
            dma((2,)),
            dma((2,)),
            dma((6,)),
            dma((4 * ROUNDS,)),
            dma((2 * ROUNDS,)),
            dma((2 * ROUNDS,)),
        ],
        compiler_params=pltpu.CompilerParams(
            collective_id=0, has_side_effects=True, vmem_limit_bytes=40 << 20
        ),
    )(*(pltpu.with_memory_space_constraint(x, pltpu.HBM) for x in (w, h, g, q)))
    new, edge = pl.pallas_call(
        write_kernel,
        out_shape=(
            jax.ShapeDtypeStruct((rows, width), BF16),
            jax.ShapeDtypeStruct((rank, width), F32),
        ),
        in_specs=[vmem] * 4,
        out_specs=(hbm, hbm),
        scratch_shapes=[pltpu.VMEM((rows, width), BF16), dma((rows // 128 + 1,))],
        compiler_params=pltpu.CompilerParams(vmem_limit_bytes=16 << 20),
    )(*(pltpu.with_memory_space_constraint(x, pltpu.VMEM) for x in parts))
    return new[None], edge.T[None]


def solution(mesh):
    placed = (
        P("blk", "fsdp", None),
        P("blk", None, "fsdp"),
        P("blk", "fsdp", None),
        P("blk", None, None),
    )
    return jax.shard_map(
        functools.partial(on_device, mesh.shape["blk"], mesh.shape["fsdp"]),
        mesh=mesh,
        in_specs=placed,
        out_specs=(P("blk", "fsdp", None), P("blk", None, None)),
        check_vma=False,
    )
```

```python
import functools
import math

import jax
import jax.numpy as jnp
from jax import lax
from jax.experimental import pallas as pl
from jax.experimental.pallas import tpu as pltpu
from jax.sharding import PartitionSpec as P

ROUNDS = 2
MESH = pl.DeviceIdType.MESH
F32, BF16 = jnp.float32, jnp.bfloat16

NT = (((1,), (1,)), ((), ()))
NN = (((1,), (0,)), ((), ()))
TN = (((0,), (0,)), ((), ()))


def mm(a, b, dims):
    return lax.dot_general(a, b, dims, preferred_element_type=F32)


def pieces(x):
    high = x.astype(BF16).astype(F32)
    rest = x - high
    mid = rest.astype(BF16).astype(F32)
    low = rest - mid
    return jnp.concatenate([high, mid, low], axis=0).astype(BF16)


def joined(y):
    n = y.shape[0] // 3
    return y[:n] + (y[n : 2 * n] + y[2 * n :])


def edge_row(x, k, first):
    return jnp.where(
        first,
        jnp.broadcast_to(x[k : k + 1], x.shape),
        jnp.broadcast_to(x[4 + k : 5 + k], x.shape),
    )


def eliminate(q, m, others):
    rows = lax.broadcasted_iota(jnp.int32, (8, 1), 0)
    first = rows < 4
    within = rows - jnp.where(first, 0, 4)
    gram = [jnp.sum(m * edge_row(q, k, first), axis=1, keepdims=True) for k in range(4)]
    arrays = [m] + others
    diagonal = jnp.zeros((8, 1), F32)
    for k in range(4):
        pivot = edge_row(gram[k], k, first)
        diagonal = jnp.where(within == k, gram[k], diagonal)
        factor = jnp.where(within > k, gram[k] / pivot, 0.0)
        if k < 3:
            for j in range(k + 1, 4):
                gram[j] = gram[j] - factor * edge_row(gram[j], k, first)
            arrays = [a - factor * edge_row(a, k, first) for a in arrays]
    scale = 1.0 / jnp.sqrt(diagonal)
    return [a * scale for a in arrays]


def kernel(n_blk, n_fsdp, step, w_hbm, h_hbm, g_hbm, q_hbm, base, left, right, edge_ref,
           w, h, g, w_t, tokens_t, g_ref, g_pad, gq, q_ref, q_left, q_all, p_send, p_recv, m_part, m_recv, m_sum,
           m_all, in_sem, q_sem, gq_sem, g_sem, p_sem, rs_sem, ag_sem):
    b, f = lax.axis_index("blk"), lax.axis_index("fsdp")
    up, down = lax.rem(b + 1, n_blk), lax.rem(b + n_blk - 1, n_blk)
    half = n_fsdp // 2
    mine = lax.rem(f, half)
    start_of_half = f - mine
    rows, width = w.shape
    strip = width // (half // 2)

    def remote(src, dst, sems, at, where):
        return pltpu.make_async_remote_copy(
            src_ref=src, dst_ref=dst, send_sem=sems.at[at], recv_sem=sems.at[at + 1],
            device_id=where, device_id_type=MESH,
        )

    def settle(ref, sem):
        pltpu.make_async_copy(ref, ref, sem).wait()

    load_w = pltpu.make_async_copy(w_hbm, w, in_sem.at[0])
    load_h = pltpu.make_async_copy(h_hbm, h, in_sem.at[1])
    load_g = pltpu.make_async_copy(g_hbm, g_ref, in_sem.at[2])
    load_q = pltpu.make_async_copy(q_hbm, q_ref, in_sem.at[3])
    for load in (load_q, load_g, load_w, load_h):
        load.start()
    others = [(b, lax.rem(f + k, n_fsdp)) for k in sorted(range(1, n_fsdp), key=lambda k: abs(k - half))]
    barrier = pltpu.get_barrier_semaphore()
    odd = lax.rem(mine, 2)
    mainly, also = jnp.where(odd == 1, up, down), jnp.where(odd == 1, down, up)
    beside = [(mainly, start_of_half + s) for s in range(half)]
    beside += [(also, start_of_half + 2 * s + odd) for s in range(half // 2)]
    for where in others + beside:
        pl.semaphore_signal(barrier, inc=1, device_id=where, device_id_type=MESH)
    pl.semaphore_wait(barrier, len(others) + len(beside))

    load_q.wait()
    load_g.wait()
    send_q = remote(q_ref, q_left, q_sem, 0, (up, f))
    send_q.start()
    mate = f + 1 - 2 * lax.rem(f, 2)

    def along_z(k):
        return lax.rem(f + 2 * k + n_fsdp, n_fsdp)

    def pass_to_mate(owners):
        for there in owners:
            remote(g.at[there], g.at[there], g_sem, 4, (b, mate)).start()

    near = [along_z(k) for k in (1, -1, 2, -2)]
    far = [along_z(k) for k in (3, -3, 4)]
    for there in near:
        remote(g_ref, g.at[f], g_sem, 0, (b, there)).start()
    remote(g_ref, g.at[f], g_sem, 4, (b, mate)).start()
    g[f] = g_ref[...]
    q_all[0:4] = q_ref[...]
    block = g_ref.shape[0]
    per_tile = g_pad.shape[0] // block
    g_pad[...] = jnp.zeros_like(g_pad)
    g_pad[pl.ds(pl.multiple_of(block * lax.rem(f, per_tile), block), block)] = g_ref[...]
    send_q.wait_recv()
    q_all[4:8] = q_left[...]
    q = q_all[...]
    gq[f] = joined(mm(pieces(q), g_pad[...], NT))
    for where in others:
        remote(gq.at[f], gq.at[f], gq_sem, 0, where).start()
    settle(g.at[pl.ds(0, len(near))], g_sem.at[1])
    for held, to in ((2, -1), (-2, 1), (2, -2)):
        held = along_z(held)
        remote(g.at[held], g.at[held], g_sem, 2, (b, along_z(to))).start()
    pass_to_mate(near)
    load_w.wait()
    load_h.wait()
    tokens = None

    for r in range(ROUNDS):
        if r == 0:
            own = joined(mm(pieces(q), w[...], NT))
            settle(gq.at[pl.ds(0, n_fsdp - 1)], gq_sem.at[1])
            seen = jnp.concatenate(
                [sum(gq[i + k] for k in range(per_tile)) for i in range(0, n_fsdp, per_tile)], axis=1
            )
        else:
            m3 = pieces(m)
            seen = joined(mm(m3, tokens_t[...], NN))
            own = joined(mm(m3, w_t[...], NN))
        own = own - joined(mm(pieces(step * seen), h[...], NN))
        if r > 0:
            q, own = eliminate(q, m, [own])
        p_send[r, 0] = own[0:4]
        p_send[r, 1] = own[4:8]
        to_up = remote(p_send.at[r, 0], p_recv.at[r, 1], p_sem, 4 * r, (up, f))
        to_down = remote(p_send.at[r, 1], p_recv.at[r, 0], p_sem, 4 * r + 2, (down, f))
        to_up.start()
        to_down.start()
        if r == 0:
            settle(g.at[pl.ds(0, len(far))], g_sem.at[3])
            pass_to_mate(far)
        to_up.wait_recv()
        to_down.wait_recv()
        p = jnp.concatenate([own[0:4] - p_recv[r, 0], p_recv[r, 1] - own[4:8]], axis=0)
        p3 = pieces(p)
        seen = joined(mm(p3, h[...], NT))
        part = joined(mm(p3, w[...], NN))
        if r == 0:
            settle(g.at[pl.ds(0, half)], g_sem.at[5])
            tokens = g[...].reshape(n_fsdp * block, width)
        part = part - joined(mm(pieces(step * seen), tokens, NN))
        for s in range(half):
            i, j = 4 - 4 * (s % 2), strip * (s // 2)
            m_part[r, s] = part[i : i + 4, j : j + strip]
        for s in range(half // 2):
            above, below = 2 * s + 1, 2 * s
            remote(m_part.at[r, above], m_recv.at[r, half + mine], rs_sem, 2 * r, (up, start_of_half + below)).start()
            remote(m_part.at[r, below], m_recv.at[r, half + mine], rs_sem, 2 * r, (down, start_of_half + above)).start()
        for k in range(1, half):
            to = lax.rem(mine + k, half)
            remote(m_part.at[r, to], m_recv.at[r, mine], rs_sem, 2 * r, (b, start_of_half + to)).start()
        m_recv[r, mine] = m_part[r, mine]
        if r == 0:
            for i in range(0, rows, 128):
                base[i : i + 128] = w[i : i + 128].astype(F32) - step * mm(h[:, i : i + 128], tokens, TN)
            w_t[...] = w[...].T
            tokens_t[...] = tokens.T
        settle(m_recv.at[r, pl.ds(0, 2 * half - 1)], rs_sem.at[2 * r + 1])
        total = m_recv[r, 0] - m_recv[r, half]
        for s in range(1, half):
            total = total + (m_recv[r, s] - m_recv[r, half + s])
        m_sum[r, f] = jnp.where(odd == 1, 1.0, -1.0) * total
        for where in others:
            remote(m_sum.at[r, f], m_sum.at[r, f], ag_sem, 2 * r, where).start()
        settle(m_sum.at[r, pl.ds(0, n_fsdp - 1)], ag_sem.at[2 * r + 1])
        for s in range(half):
            i, j = 4 - 4 * (s % 2), strip * (s // 2)
            m_all[i : i + 4, j : j + strip] = m_sum[r, s] + m_sum[r, half + s]
        m = m_all[...]

    q, p = eliminate(q, m, [p])
    edge_ref[...] = q[0:4]
    sign = jnp.where(lax.broadcasted_iota(jnp.int32, (8, 1), 0) < 4, -0.5, 0.5)
    q3, p3 = pieces(q), pieces(sign * p)
    left[...] = jnp.concatenate([p3[0:8], p3[0:8], p3[8:16], p3[0:8], p3[16:24], p3[8:16]], axis=0)
    right[...] = jnp.concatenate([q3[0:8], q3[8:16], q3[0:8], q3[16:24], q3[0:8], q3[8:16]], axis=0)

    send_q.wait_send()
    settle(gq.at[pl.ds(0, n_fsdp - 1)], gq_sem.at[0])
    settle(g.at[pl.ds(0, len(near))], g_sem.at[0])
    settle(g.at[pl.ds(0, len(far))], g_sem.at[2])
    settle(g.at[pl.ds(0, half)], g_sem.at[4])
    for r in range(ROUNDS):
        settle(p_send.at[r, 0], p_sem.at[4 * r])
        settle(p_send.at[r, 1], p_sem.at[4 * r + 2])
        settle(m_recv.at[r, pl.ds(0, 2 * half - 1)], rs_sem.at[2 * r])
        settle(m_sum.at[r, pl.ds(0, n_fsdp - 1)], ag_sem.at[2 * r])


def write_kernel(base, left, right, edge, new_hbm, edge_hbm, new, sem):
    saves = [pltpu.make_async_copy(edge, edge_hbm, sem.at[0])]
    saves[0].start()
    for n, i in enumerate(range(0, base.shape[0], 128)):
        at = pl.ds(i, 128)
        new[at] = (base[at] + mm(left[:, at], right[...], TN)).astype(BF16)
        saves.append(pltpu.make_async_copy(new.at[at], new_hbm.at[at], sem.at[1 + n]))
        saves[-1].start()
    for save in saves:
        save.wait()


def on_device(n_blk, n_fsdp, weights, hidden, out_grad, q_start):
    w, h, g, q = weights[0], hidden[0], out_grad[0], q_start[0].T
    rows, width = w.shape
    tokens = h.shape[0]
    rank = q.shape[0]
    half = n_fsdp // 2
    strip = width // (half // 2)
    dma = pltpu.SemaphoreType.DMA
    vmem = pl.BlockSpec(memory_space=pltpu.VMEM)
    hbm = pl.BlockSpec(memory_space=pl.ANY)
    parts = pl.pallas_call(
        functools.partial(kernel, n_blk, n_fsdp, 0.5 / math.sqrt(tokens)),
        out_shape=(
            pltpu.VMEM((rows, width), F32),
            pltpu.VMEM((12 * rank, rows), BF16),
            pltpu.VMEM((12 * rank, width), BF16),
            pltpu.VMEM((rank, width), F32),
        ),
        in_specs=[hbm, hbm, hbm, hbm],
        out_specs=(vmem, vmem, vmem, vmem),
        scratch_shapes=[
            pltpu.VMEM((rows, width), BF16),
            pltpu.VMEM((tokens, rows), BF16),
            pltpu.VMEM((n_fsdp, tokens // n_fsdp, width), BF16),
            pltpu.VMEM((width, rows), BF16),
            pltpu.VMEM((width, tokens), BF16),
            pltpu.VMEM((tokens // n_fsdp, width), BF16),
            pltpu.VMEM((128, width), BF16),
            pltpu.VMEM((n_fsdp, 2 * rank, 128), F32),
            pltpu.VMEM((rank, width), F32),
            pltpu.VMEM((rank, width), F32),
            pltpu.VMEM((2 * rank, width), F32),
            pltpu.VMEM((ROUNDS, 2, rank, rows), F32),
            pltpu.VMEM((ROUNDS, 2, rank, rows), F32),
            pltpu.VMEM((ROUNDS, half, rank, strip), F32),
            pltpu.VMEM((ROUNDS, 2 * half, rank, strip), F32),
            pltpu.VMEM((ROUNDS, n_fsdp, rank, strip), F32),
            pltpu.VMEM((2 * rank, width), F32),
            dma((4,)),
            dma((2,)),
            dma((2,)),
            dma((6,)),
            dma((4 * ROUNDS,)),
            dma((2 * ROUNDS,)),
            dma((2 * ROUNDS,)),
        ],
        compiler_params=pltpu.CompilerParams(
            collective_id=0, has_side_effects=True, vmem_limit_bytes=40 << 20
        ),
    )(*(pltpu.with_memory_space_constraint(x, pltpu.HBM) for x in (w, h, g, q)))
    new, edge = pl.pallas_call(
        write_kernel,
        out_shape=(
            jax.ShapeDtypeStruct((rows, width), BF16),
            jax.ShapeDtypeStruct((rank, width), F32),
        ),
        in_specs=[vmem] * 4,
        out_specs=(hbm, hbm),
        scratch_shapes=[pltpu.VMEM((rows, width), BF16), dma((rows // 128 + 1,))],
        compiler_params=pltpu.CompilerParams(vmem_limit_bytes=16 << 20),
    )(*(pltpu.with_memory_space_constraint(x, pltpu.VMEM) for x in parts))
    return new[None], edge.T[None]


def solution(mesh):
    placed = (
        P("blk", "fsdp", None),
        P("blk", None, "fsdp"),
        P("blk", "fsdp", None),
        P("blk", None, None),
    )
    return jax.shard_map(
        functools.partial(on_device, mesh.shape["blk"], mesh.shape["fsdp"]),
        mesh=mesh,
        in_specs=placed,
        out_specs=(P("blk", "fsdp", None), P("blk", None, None)),
        check_vma=False,
    )
```

```python
import functools
import math

import jax
import jax.numpy as jnp
from jax import lax
from jax.experimental import pallas as pl
from jax.experimental.pallas import tpu as pltpu
from jax.sharding import PartitionSpec as P

ROUNDS = 2
MESH = pl.DeviceIdType.MESH
F32, BF16 = jnp.float32, jnp.bfloat16

NT = (((1,), (1,)), ((), ()))
NN = (((1,), (0,)), ((), ()))
TN = (((0,), (0,)), ((), ()))


def mm(a, b, dims):
    return lax.dot_general(a, b, dims, preferred_element_type=F32)


def pieces(x):
    high = x.astype(BF16).astype(F32)
    rest = x - high
    mid = rest.astype(BF16).astype(F32)
    low = rest - mid
    return jnp.concatenate([high, mid, low], axis=0).astype(BF16)


def joined(y):
    n = y.shape[0] // 3
    return y[:n] + (y[n : 2 * n] + y[2 * n :])


def edge_row(x, k, first):
    return jnp.where(
        first,
        jnp.broadcast_to(x[k : k + 1], x.shape),
        jnp.broadcast_to(x[4 + k : 5 + k], x.shape),
    )


def eliminate(q, m, others):
    rows = lax.broadcasted_iota(jnp.int32, (8, 1), 0)
    first = rows < 4
    within = rows - jnp.where(first, 0, 4)
    gram = [jnp.sum(m * edge_row(q, k, first), axis=1, keepdims=True) for k in range(4)]
    arrays = [m] + others
    diagonal = jnp.zeros((8, 1), F32)
    for k in range(4):
        pivot = edge_row(gram[k], k, first)
        diagonal = jnp.where(within == k, gram[k], diagonal)
        factor = jnp.where(within > k, gram[k] / pivot, 0.0)
        if k < 3:
            for j in range(k + 1, 4):
                gram[j] = gram[j] - factor * edge_row(gram[j], k, first)
            arrays = [a - factor * edge_row(a, k, first) for a in arrays]
    scale = 1.0 / jnp.sqrt(diagonal)
    return [a * scale for a in arrays]


def kernel(n_blk, n_fsdp, step, w_hbm, h_hbm, g_hbm, q_hbm, base, left, right, edge_ref,
           w, h, g, w_t, tokens_t, g_ref, g_pad, gq, q_ref, q_left, q_all, p_send, p_recv, m_part, m_recv, m_sum,
           m_all, in_sem, q_sem, gq_sem, g_sem, p_sem, rs_sem, ag_sem):
    b, f = lax.axis_index("blk"), lax.axis_index("fsdp")
    up, down = lax.rem(b + 1, n_blk), lax.rem(b + n_blk - 1, n_blk)
    half = n_fsdp // 2
    mine = lax.rem(f, half)
    start_of_half = f - mine
    rows, width = w.shape
    strip = width // (half // 2)

    def remote(src, dst, sems, at, where):
        return pltpu.make_async_remote_copy(
            src_ref=src, dst_ref=dst, send_sem=sems.at[at], recv_sem=sems.at[at + 1],
            device_id=where, device_id_type=MESH,
        )

    def settle(ref, sem):
        pltpu.make_async_copy(ref, ref, sem).wait()

    load_w = pltpu.make_async_copy(w_hbm, w, in_sem.at[0])
    load_h = pltpu.make_async_copy(h_hbm, h, in_sem.at[1])
    load_g = pltpu.make_async_copy(g_hbm, g_ref, in_sem.at[2])
    load_q = pltpu.make_async_copy(q_hbm, q_ref, in_sem.at[3])
    for load in (load_q, load_g, load_w, load_h):
        load.start()
    others = [(b, lax.rem(f + k, n_fsdp)) for k in sorted(range(1, n_fsdp), key=lambda k: abs(k - half))]
    barrier = pltpu.get_barrier_semaphore()
    odd = lax.rem(mine, 2)
    mainly, also = jnp.where(odd == 1, up, down), jnp.where(odd == 1, down, up)
    beside = [(mainly, start_of_half + s) for s in range(half)]
    beside += [(also, start_of_half + 2 * s + odd) for s in range(half // 2)]
    for where in beside + others:
        pl.semaphore_signal(barrier, inc=1, device_id=where, device_id_type=MESH)
    pl.semaphore_wait(barrier, len(others) + len(beside))

    load_q.wait()
    send_q = remote(q_ref, q_left, q_sem, 0, (up, f))
    send_q.start()
    load_g.wait()
    mate = f + 1 - 2 * lax.rem(f, 2)

    def along_z(k):
        return lax.rem(f + 2 * k + n_fsdp, n_fsdp)

    def pass_to_mate(owners):
        for there in owners:
            remote(g.at[there], g.at[there], g_sem, 4, (b, mate)).start()

    near = [along_z(k) for k in (1, -1, 2, -2)]
    far = [along_z(k) for k in (3, -3, 4)]
    for there in near:
        remote(g_ref, g.at[f], g_sem, 0, (b, there)).start()
    remote(g_ref, g.at[f], g_sem, 4, (b, mate)).start()
    g[f] = g_ref[...]
    q_all[0:4] = q_ref[...]
    block = g_ref.shape[0]
    per_tile = g_pad.shape[0] // block
    g_pad[...] = jnp.zeros_like(g_pad)
    g_pad[pl.ds(pl.multiple_of(block * lax.rem(f, per_tile), block), block)] = g_ref[...]
    send_q.wait_recv()
    q_all[4:8] = q_left[...]
    q = q_all[...]
    gq[f] = joined(mm(pieces(q), g_pad[...], NT))
    for where in others:
        remote(gq.at[f], gq.at[f], gq_sem, 0, where).start()
    settle(g.at[pl.ds(0, len(near))], g_sem.at[1])
    for held, to in ((2, -1), (-2, 1), (2, -2)):
        held = along_z(held)
        remote(g.at[held], g.at[held], g_sem, 2, (b, along_z(to))).start()
    pass_to_mate(near)
    load_w.wait()
    load_h.wait()
    tokens = None

    for r in range(ROUNDS):
        if r == 0:
            own = joined(mm(pieces(q), w[...], NT))
            settle(gq.at[pl.ds(0, n_fsdp - 1)], gq_sem.at[1])
            seen = jnp.concatenate(
                [sum(gq[i + k] for k in range(per_tile)) for i in range(0, n_fsdp, per_tile)], axis=1
            )
        else:
            m3 = pieces(m)
            seen = joined(mm(m3, tokens_t[...], NN))
            own = joined(mm(m3, w_t[...], NN))
        own = own - joined(mm(pieces(step * seen), h[...], NN))
        if r > 0:
            q, own = eliminate(q, m, [own])
        p_send[r, 0] = own[0:4]
        p_send[r, 1] = own[4:8]
        to_up = remote(p_send.at[r, 0], p_recv.at[r, 1], p_sem, 4 * r, (up, f))
        to_down = remote(p_send.at[r, 1], p_recv.at[r, 0], p_sem, 4 * r + 2, (down, f))
        to_up.start()
        to_down.start()
        if r == 0:
            settle(g.at[pl.ds(0, len(far))], g_sem.at[3])
            pass_to_mate(far)
        to_up.wait_recv()
        to_down.wait_recv()
        p = jnp.concatenate([own[0:4] - p_recv[r, 0], p_recv[r, 1] - own[4:8]], axis=0)
        p3 = pieces(p)
        seen = joined(mm(p3, h[...], NT))
        part = joined(mm(p3, w[...], NN))
        if r == 0:
            settle(g.at[pl.ds(0, half)], g_sem.at[5])
            tokens = g[...].reshape(n_fsdp * block, width)
        part = part - joined(mm(pieces(step * seen), tokens, NN))
        for s in range(half):
            i, j = 4 - 4 * (s % 2), strip * (s // 2)
            m_part[r, s] = part[i : i + 4, j : j + strip]
        for s in range(half // 2):
            above, below = 2 * s + 1, 2 * s
            remote(m_part.at[r, above], m_recv.at[r, half + mine], rs_sem, 2 * r, (up, start_of_half + below)).start()
            remote(m_part.at[r, below], m_recv.at[r, half + mine], rs_sem, 2 * r, (down, start_of_half + above)).start()
        for k in range(1, half):
            to = lax.rem(mine + k, half)
            remote(m_part.at[r, to], m_recv.at[r, mine], rs_sem, 2 * r, (b, start_of_half + to)).start()
        m_recv[r, mine] = m_part[r, mine]
        if r == 0:
            for i in range(0, rows, 128):
                base[i : i + 128] = w[i : i + 128].astype(F32) - step * mm(h[:, i : i + 128], tokens, TN)
            w_t[...] = w[...].T
            tokens_t[...] = tokens.T
        settle(m_recv.at[r, pl.ds(0, 2 * half - 1)], rs_sem.at[2 * r + 1])
        total = m_recv[r, 0] - m_recv[r, half]
        for s in range(1, half):
            total = total + (m_recv[r, s] - m_recv[r, half + s])
        m_sum[r, f] = jnp.where(odd == 1, 1.0, -1.0) * total
        for where in others:
            remote(m_sum.at[r, f], m_sum.at[r, f], ag_sem, 2 * r, where).start()
        settle(m_sum.at[r, pl.ds(0, n_fsdp - 1)], ag_sem.at[2 * r + 1])
        for s in range(half):
            i, j = 4 - 4 * (s % 2), strip * (s // 2)
            m_all[i : i + 4, j : j + strip] = m_sum[r, s] + m_sum[r, half + s]
        m = m_all[...]

    q, p = eliminate(q, m, [p])
    edge_ref[...] = q[0:4]
    sign = jnp.where(lax.broadcasted_iota(jnp.int32, (8, 1), 0) < 4, -0.5, 0.5)
    q3, p3 = pieces(q), pieces(sign * p)
    left[...] = jnp.concatenate([p3[0:8], p3[0:8], p3[8:16], p3[0:8], p3[16:24], p3[8:16]], axis=0)
    right[...] = jnp.concatenate([q3[0:8], q3[8:16], q3[0:8], q3[16:24], q3[0:8], q3[8:16]], axis=0)

    send_q.wait_send()
    settle(gq.at[pl.ds(0, n_fsdp - 1)], gq_sem.at[0])
    settle(g.at[pl.ds(0, len(near))], g_sem.at[0])
    settle(g.at[pl.ds(0, len(far))], g_sem.at[2])
    settle(g.at[pl.ds(0, half)], g_sem.at[4])
    for r in range(ROUNDS):
        settle(p_send.at[r, 0], p_sem.at[4 * r])
        settle(p_send.at[r, 1], p_sem.at[4 * r + 2])
        settle(m_recv.at[r, pl.ds(0, 2 * half - 1)], rs_sem.at[2 * r])
        settle(m_sum.at[r, pl.ds(0, n_fsdp - 1)], ag_sem.at[2 * r])


def write_kernel(base, left, right, edge, new_hbm, edge_hbm, new, sem):
    saves = [pltpu.make_async_copy(edge, edge_hbm, sem.at[0])]
    saves[0].start()
    for n, i in enumerate(range(0, base.shape[0], 128)):
        at = pl.ds(i, 128)
        new[at] = (base[at] + mm(left[:, at], right[...], TN)).astype(BF16)
        saves.append(pltpu.make_async_copy(new.at[at], new_hbm.at[at], sem.at[1 + n]))
        saves[-1].start()
    for save in saves:
        save.wait()


def on_device(n_blk, n_fsdp, weights, hidden, out_grad, q_start):
    w, h, g, q = weights[0], hidden[0], out_grad[0], q_start[0].T
    rows, width = w.shape
    tokens = h.shape[0]
    rank = q.shape[0]
    half = n_fsdp // 2
    strip = width // (half // 2)
    dma = pltpu.SemaphoreType.DMA
    vmem = pl.BlockSpec(memory_space=pltpu.VMEM)
    hbm = pl.BlockSpec(memory_space=pl.ANY)
    parts = pl.pallas_call(
        functools.partial(kernel, n_blk, n_fsdp, 0.5 / math.sqrt(tokens)),
        out_shape=(
            pltpu.VMEM((rows, width), F32),
            pltpu.VMEM((12 * rank, rows), BF16),
            pltpu.VMEM((12 * rank, width), BF16),
            pltpu.VMEM((rank, width), F32),
        ),
        in_specs=[hbm, hbm, hbm, hbm],
        out_specs=(vmem, vmem, vmem, vmem),
        scratch_shapes=[
            pltpu.VMEM((rows, width), BF16),
            pltpu.VMEM((tokens, rows), BF16),
            pltpu.VMEM((n_fsdp, tokens // n_fsdp, width), BF16),
            pltpu.VMEM((width, rows), BF16),
            pltpu.VMEM((width, tokens), BF16),
            pltpu.VMEM((tokens // n_fsdp, width), BF16),
            pltpu.VMEM((128, width), BF16),
            pltpu.VMEM((n_fsdp, 2 * rank, 128), F32),
            pltpu.VMEM((rank, width), F32),
            pltpu.VMEM((rank, width), F32),
            pltpu.VMEM((2 * rank, width), F32),
            pltpu.VMEM((ROUNDS, 2, rank, rows), F32),
            pltpu.VMEM((ROUNDS, 2, rank, rows), F32),
            pltpu.VMEM((ROUNDS, half, rank, strip), F32),
            pltpu.VMEM((ROUNDS, 2 * half, rank, strip), F32),
            pltpu.VMEM((ROUNDS, n_fsdp, rank, strip), F32),
            pltpu.VMEM((2 * rank, width), F32),
            dma((4,)),
            dma((2,)),
            dma((2,)),
            dma((6,)),
            dma((4 * ROUNDS,)),
            dma((2 * ROUNDS,)),
            dma((2 * ROUNDS,)),
        ],
        compiler_params=pltpu.CompilerParams(
            collective_id=0, has_side_effects=True, vmem_limit_bytes=40 << 20
        ),
    )(*(pltpu.with_memory_space_constraint(x, pltpu.HBM) for x in (w, h, g, q)))
    new, edge = pl.pallas_call(
        write_kernel,
        out_shape=(
            jax.ShapeDtypeStruct((rows, width), BF16),
            jax.ShapeDtypeStruct((rank, width), F32),
        ),
        in_specs=[vmem] * 4,
        out_specs=(hbm, hbm),
        scratch_shapes=[pltpu.VMEM((rows, width), BF16), dma((rows // 128 + 1,))],
        compiler_params=pltpu.CompilerParams(vmem_limit_bytes=16 << 20),
    )(*(pltpu.with_memory_space_constraint(x, pltpu.VMEM) for x in parts))
    return new[None], edge.T[None]


def solution(mesh):
    placed = (
        P("blk", "fsdp", None),
        P("blk", None, "fsdp"),
        P("blk", "fsdp", None),
        P("blk", None, None),
    )
    return jax.shard_map(
        functools.partial(on_device, mesh.shape["blk"], mesh.shape["fsdp"]),
        mesh=mesh,
        in_specs=placed,
        out_specs=(P("blk", "fsdp", None), P("blk", None, None)),
        check_vma=False,
    )
```
